256 devices in a mesh: band: 32 (over z, x_hi, core), slab: 8 (over x_lo, y).
Axes of the slice: x: 4 (x_hi: 2, x_lo: 2; x = x_hi * 2 + x_lo), y: 4, z: 8, core: 2. Of those that a mesh axis runs over, the one named last changes fastest.
Arguments:
- orbital: float32 [32, 128, 128, 128], P('band', 'slab'), may hold values from -18 to 18
- potential: float32 [128, 128, 128], P('slab', 'band'), may hold values from -4 to 2
Outputs:
- filtered: float32 [32, 128, 128, 128], P('band', 'slab')
The draws below stay inside these ranges and needn't reach their ends.
All inputs are finite; a program needn't handle non-finite values.
Results may differ from the reference program's by a relative error of at most 0.00002.
Values sent between devices are 32-bit elements; how exact they have to be, the bound alone decides.
No kernel may reach another device: no remote copies, remote signals or barrier semaphores. Data moves between devices by JAX's collectives and lax.ppermute only.
A program may use at most 64 MiB of HBM per device.

```python
import jax
import jax.numpy as jnp

NY = 128
NZ = 128
DEGREE = 3
NX = 128
BANDS = 32


def block_levels(rng, shape, shards, low, largest):
    loudness, own = 1.0, jax.random.fold_in(rng, 6)
    for axis_at, blocks in shards:
        steps = jnp.exp(jax.random.uniform(jax.random.fold_in(own, axis_at), (blocks,), jnp.float32, low / len(shards), largest / len(shards)))
        loudness = loudness * jnp.repeat(steps, shape[axis_at] // blocks).reshape([-1 if axis == axis_at else 1 for axis in range(len(shape))])
    return loudness


def normal_values(rng, shape, deviation, most, pieces=(), held_as=jnp.bfloat16):
    values = deviation * jax.random.normal(rng, shape, jnp.float32)
    if pieces:
        values = values * block_levels(rng, shape, pieces, -0.22, 0.18)
    return jnp.clip(values, -most, most).astype(held_as)


def setup_inputs(seed: int = 0) -> dict:
    streams_of = jax.random.split(jax.random.key(seed), 3)
    orbital = normal_values(streams_of[0], (BANDS, NX, NY, NZ), 3.0, 18.0, ((0, 32), (1, 8)), jnp.float32)
    potential = jnp.clip(-4.0 + 6.0 * jax.random.uniform(streams_of[1], (NX, NY, NZ), jnp.float32) ** block_levels(streams_of[1], (NX, NY, NZ), ((0, 8), (1, 32)), -0.2, 0.2), -4.0, 2.0)
    return {"orbital": orbital, "potential": potential}


COEFS = (-5369.0 / 1800.0, 12.0 / 7.0, -15.0 / 56.0, 10.0 / 189.0, -1.0 / 112.0, 2.0 / 1925.0, -1.0 / 16632.0)
INVERSE_SQ = 1.0 / 0.64
UPPER_HALF = 10.0
CENTER = 10.0
FLOOR = -5.0


def hamiltonian(field, potential):
    total = 3.0 * COEFS[0] * field
    for shift in range(1, 7):
        for axis in range(3):
            total = total + COEFS[shift] * (jnp.roll(field, shift, axis) + jnp.roll(field, -shift, axis))
    return -0.5 * INVERSE_SQ * total + potential * field


def filter_one(orbit, potential):
    sigma_one = UPPER_HALF / (FLOOR - CENTER)
    gamma = 2.0 / sigma_one
    older = orbit
    newer = (sigma_one / UPPER_HALF) * (hamiltonian(older, potential) - CENTER * older)
    sigma = sigma_one
    for step in range(DEGREE - 1):
        tnext = 1.0 / (gamma - sigma)
        image = hamiltonian(newer, potential)
        fresh = (2.0 * tnext / UPPER_HALF) * (image - CENTER * newer) - (sigma * tnext) * older
        older, newer = newer, fresh
        sigma = tnext
    return newer


def reference(orbital, potential):
    return jax.lax.map(lambda orbit: filter_one(orbit, potential), orbital)
```

```python
import functools

import jax
import jax.numpy as jnp
import ml_dtypes
import numpy as np
from jax import lax
from jax.experimental import pallas as pl
from jax.experimental.pallas import tpu as pltpu
from jax.sharding import PartitionSpec as P

DEGREE = 3
COEFS = (
    -5369.0 / 1800.0,
    12.0 / 7.0,
    -15.0 / 56.0,
    10.0 / 189.0,
    -1.0 / 112.0,
    2.0 / 1925.0,
    -1.0 / 16632.0,
)
INVERSE_SQ = 1.0 / 0.64
UPPER_HALF = 10.0
CENTER = 10.0
FLOOR = -5.0

KIN = tuple(-0.5 * INVERSE_SQ * c for c in COEFS)
SIGMA1 = UPPER_HALF / (FLOOR - CENTER)
GAMMA = 2.0 / SIGMA1
SIGMA2 = 1.0 / (GAMMA - SIGMA1)
SIGMA3 = 1.0 / (GAMMA - SIGMA2)
STEP1 = (SIGMA1 / UPPER_HALF, None)
STEP2 = (2.0 * SIGMA2 / UPPER_HALF, SIGMA1 * SIGMA2)
STEP3 = (2.0 * SIGMA3 / UPPER_HALF, SIGMA2 * SIGMA3)

W = 6
F32 = jnp.float32
BF16 = jnp.bfloat16
SLOTS_S = ((0, 0), (0, 1), (3, 0), (3, 1), (-3, 0), (-3, 1))
SLOTS_U = tuple((dz + 1, dh) for dz, dh in SLOTS_S)
SLOTS_D = tuple((dz - 1, dh) for dz, dh in SLOTS_S[:4])
SLOTS = SLOTS_S + SLOTS_U + SLOTS_D


def circulant(n):
    dense = np.zeros((n, n), np.float64)
    for k in range(1, W + 1):
        for i in range(n):
            dense[i, (i + k) % n] += KIN[k]
            dense[i, (i - k) % n] += KIN[k]
    high = dense.astype(ml_dtypes.bfloat16)
    low = (dense - high.astype(np.float64)).astype(ml_dtypes.bfloat16)
    return np.block([[high, low], [high, low]])


def in_planes(planes, left, right, out):
    n = left.shape[0] // 2
    for i in range(0, len(planes), 2):
        pair = [planes[i][...], planes[i + 1][...]]
        high = [f.astype(BF16) for f in pair]
        low = [(f - h.astype(F32)).astype(BF16) for f, h in zip(pair, high)]
        tall = jnp.concatenate([jnp.concatenate(high, 1), jnp.concatenate(low, 1)], 0)
        wide = jnp.concatenate([jnp.concatenate(high, 0), jnp.concatenate(low, 0)], 1)
        along_y = jnp.dot(left[...], tall, preferred_element_type=F32)
        along_z = jnp.dot(wide, right[...], preferred_element_type=F32)
        along_y = along_y[:n] + along_y[n:]
        along_z = along_z[:, :n] + along_z[:, n:]
        out[i] = along_y[:, :n] + along_z[:n]
        out[i + 1] = along_y[:, n:] + along_z[n:]


def over_tiles(n, body):
    def step(t, carry):
        body(pl.ds(pl.multiple_of(t * 8, 8), 8))
        return carry

    lax.fori_loop(0, n // 8, step, 0)


def along_x(vals, at, scale, total):
    for k in range(1, W + 1):
        below, above = vals.get(at - k), vals.get(at + k)
        if below is None and above is None:
            continue
        near = above if below is None else (below if above is None else below + above)
        total = total + (scale * KIN[k]) * near
    return total


def place_potential(own_refs, other_refs, slots_of, planes, out):
    me = lax.axis_index("band")
    z, h, c = me // 4, (me // 2) % 2, me % 2
    mine_first = c == 0
    for own, other, slots in zip(own_refs, other_refs, slots_of):
        for i, (dz, dh) in enumerate(slots):
            zz = lax.rem(z + (dz + 8), 8)
            hh = (h + dh) % 2
            rows = pl.ds(pl.multiple_of(zz * 16 + hh * 8, 8), 8)
            for q in range(planes // 2):
                a = own[i, 8 * q : 8 * q + 8, :]
                b = other[i, 8 * q : 8 * q + 8, :]
                first = jnp.where(mine_first, a, b)
                second = jnp.where(mine_first, b, a)
                out[2 * q, rows, :] = jnp.concatenate([first[:4], second[:4]], 0)
                out[2 * q + 1, rows, :] = jnp.concatenate([first[4:], second[4:]], 0)


def kernel_own(x, left, right, w1, flat):
    in_planes([x.at[p] for p in range(16)], left, right, flat)

    def body(rows):
        vals = {p: x[p, rows, :] for p in range(16)}
        for p in range(16):
            total = flat[p, rows, :] + (3.0 * KIN[0] - CENTER) * vals[p]
            w1[p, rows, :] = along_x(vals, p, 1.0, total)

    over_tiles(x.shape[1], body)


def kernel_first(x, w1, xl, xr, s0, u0, d0, s1, u1, d1, y1, to_left, to_right, vown):
    place_potential((s0, u0, d0), (s1, u1, d1), (SLOTS_S, SLOTS_U, SLOTS_D), 16, vown)
    alpha = STEP1[0]

    def body(rows):
        vals = {p - 12: xl[p, rows, :] for p in range(6, 12)}
        vals.update({p + 16: xr[p, rows, :] for p in range(6)})
        for p in range(16):
            total = w1[p, rows, :] + vown[p, rows, :] * x[p, rows, :]
            value = alpha * along_x(vals, p, 1.0, total)
            y1[p, rows, :] = value
            if 6 <= p < 12:
                to_left[p - 6, rows, :] = value
            if 4 <= p < 10:
                to_right[p - 4, rows, :] = value

    over_tiles(x.shape[1], body)


def kernel_middle(
    x, xl, xr, y1, left, right, vown, hl0, hr0, hl1, hr1, y2l, y2r, y3, y1l, y1r, y2, vl, vr, flat
):
    n = x.shape[1]
    place_potential((hl0,), (hl1,), (SLOTS,), W, vl)
    place_potential((hr0,), (hr1,), (SLOTS,), W, vr)

    def x_at(p, rows):
        return xl[p + 12, rows, :] if p < 0 else (x[p, rows, :] if p < 16 else xr[p - 16, rows, :])

    def y1_at(p, rows):
        return y1l[p + 6, rows, :] if p < 0 else (y1[p, rows, :] if p < 16 else y1r[p - 16, rows, :])

    sides = ((-6, y1l, vl, y2l), (16, y1r, vr, y2r))
    in_planes([xl.at[p + 6] for p in range(6)] + [xr.at[p] for p in range(6)], left, right, flat)

    def first_sides(rows):
        for s, (start, dest, pot, _) in enumerate(sides):
            vals = {p: x_at(p, rows) for p in range(start - 6, start + 12)}
            for j in range(6):
                mid = vals[start + j]
                total = flat[6 * s + j, rows, :] + (pot[j, rows, :] + (3.0 * KIN[0] - CENTER)) * mid
                dest[j, rows, :] = STEP1[0] * along_x(vals, start + j, 1.0, total)

    over_tiles(n, first_sides)

    alpha, beta = STEP2
    in_planes([y1.at[p] for p in range(16)], left, right, flat)

    def second(rows):
        vals = {p: y1_at(p, rows) for p in range(-6, 22)}
        for p in range(16):
            total = flat[p, rows, :] + (vown[p, rows, :] + (3.0 * KIN[0] - CENTER)) * vals[p]
            y2[p, rows, :] = alpha * along_x(vals, p, 1.0, total) - beta * x[p, rows, :]

    over_tiles(n, second)
    in_planes([y1l.at[p] for p in range(6)] + [y1r.at[p] for p in range(6)], left, right, flat)

    def second_sides(rows):
        for s, (start, source, pot, dest) in enumerate(sides):
            low = max(start - 6, -6)
            vals = {p: y1_at(p, rows) for p in range(low, min(start + 12, 22))}
            for j in range(6):
                total = flat[6 * s + j, rows, :] + (pot[j, rows, :] + (3.0 * KIN[0] - CENTER)) * vals[start + j]
                dest[j, rows, :] = alpha * along_x(vals, start + j, 1.0, total) - beta * x_at(start + j, rows)

    over_tiles(n, second_sides)
    alpha3, beta3 = STEP3
    in_planes([y2.at[p] for p in range(16)], left, right, flat)

    def third(rows):
        vals = {p: y2[p, rows, :] for p in range(16)}
        for p in range(16):
            total = flat[p, rows, :] + (vown[p, rows, :] + (3.0 * KIN[0] - CENTER)) * vals[p]
            y3[p, rows, :] = alpha3 * along_x(vals, p, 1.0, total) - beta3 * y1[p, rows, :]

    over_tiles(n, third)


def kernel_last(far_l, far_r, y2l, y2r, y3, out):
    def body(rows):
        far = {p - 12: far_l[p, rows, :] for p in range(6)}
        far.update({p + 22: far_r[p, rows, :] for p in range(6)})
        near = {}
        for j in range(6):
            near[j - 6] = along_x(far, j - 6, STEP2[0], y2l[j, rows, :])
            near[j + 16] = along_x(far, j + 16, STEP2[0], y2r[j, rows, :])
        for p in range(16):
            out[p, rows, :] = along_x(near, p, STEP3[0], y3[p, rows, :])

    over_tiles(out.shape[1], body)


def call(body, outs, scratch, args, flops):
    whole = pl.BlockSpec(memory_space=pltpu.VMEM)
    total = sum(a.size * a.dtype.itemsize for a in args) + sum(4 * int(np.prod(o)) for o in outs)
    return pl.pallas_call(
        body,
        out_shape=tuple(jax.ShapeDtypeStruct(o, F32) for o in outs),
        in_specs=[whole] * len(args),
        out_specs=tuple(whole for _ in outs),
        scratch_shapes=[pltpu.VMEM(s, F32) for s in scratch],
        compiler_params=pltpu.CompilerParams(vmem_limit_bytes=40 * 1024 * 1024),
        cost_estimate=pl.CostEstimate(flops=flops, bytes_accessed=total, transcendentals=0),
    )(*args)


def shards(orbital, potential):
    x = orbital[0]
    nx, ny, nz = x.shape
    bands, slabs = lax.axis_size("band"), lax.axis_size("slab")
    up = [(i, (i + 1) % slabs) for i in range(slabs)]
    down = [(b, a) for a, b in up]

    def from_z(value, d):
        return lax.ppermute(value, "band", [((i + 4 * d) % bands, i) for i in range(bands)])

    def flip(value, bit):
        return lax.ppermute(value, "band", [(i ^ bit, i) for i in range(bands)])

    plane = (ny, nz)
    block = potential.reshape(1, nx * potential.shape[1], nz)
    last, first, block = lax.optimization_barrier((x[nx - 12 :], x[:12], block))
    xl = lax.ppermute(last, "slab", up)
    xr = lax.ppermute(first, "slab", down)

    s0 = jnp.concatenate([block, flip(block, 2)], 0)
    s0 = jnp.concatenate([s0, from_z(s0, 3), from_z(s0, -3)], 0)
    u0, d0 = from_z(s0, 1), from_z(s0[:4], -1)
    s1, u1, d1 = flip(s0, 1), flip(u0, 1), flip(d0, 1)
    gathered = (s0, u0, d0)
    hl0 = lax.ppermute(jnp.concatenate([g[:, 40:] for g in gathered], 0), "slab", up)
    hr0 = lax.ppermute(jnp.concatenate([g[:, :24] for g in gathered], 0), "slab", down)
    hl1, hr1 = flip(hl0, 1), flip(hr0, 1)

    mat = circulant(ny)
    right = jnp.asarray(mat)
    left = jnp.asarray(np.ascontiguousarray(mat.T))
    cells = nx * ny * nz
    six, own = (6, *plane), (16, *plane)
    (w1,) = call(kernel_own, [own], [own], [x, left, right], 40 * cells)
    y1, to_left, to_right, vown = call(
        kernel_first, [own, six, six, own], [], [x, w1, xl, xr, s0, u0, d0, s1, u1, d1], 10 * cells
    )
    far_r = lax.ppermute(to_left, "slab", down)
    far_l = lax.ppermute(to_right, "slab", up)
    y2l, y2r, y3 = call(
        kernel_middle,
        [six, six, own],
        [six, six, own, six, six, own],
        [x, xl, xr, y1, left, right, vown, hl0, hr0, hl1, hr1],
        140 * cells,
    )
    (out,) = call(kernel_last, [own], [], [far_l, far_r, y2l, y2r, y3], 10 * cells)
    return out[None]


def solution(mesh):
    placed = (P("band", "slab", None, None), P("slab", "band", None))
    return jax.shard_map(
        shards, mesh=mesh, in_specs=placed, out_specs=P("band", "slab", None, None), check_vma=False
    )
```

```python
import jax
import jax.numpy as jnp
import ml_dtypes
import numpy as np
from jax import lax
from jax.experimental import pallas as pl
from jax.experimental.pallas import tpu as pltpu
from jax.sharding import PartitionSpec as P

DEGREE = 3
COEFS = (
    -5369.0 / 1800.0,
    12.0 / 7.0,
    -15.0 / 56.0,
    10.0 / 189.0,
    -1.0 / 112.0,
    2.0 / 1925.0,
    -1.0 / 16632.0,
)
INVERSE_SQ = 1.0 / 0.64
UPPER_HALF = 10.0
CENTER = 10.0
FLOOR = -5.0

KIN = tuple(-0.5 * INVERSE_SQ * c for c in COEFS)
SIGMA1 = UPPER_HALF / (FLOOR - CENTER)
GAMMA = 2.0 / SIGMA1
SIGMA2 = 1.0 / (GAMMA - SIGMA1)
SIGMA3 = 1.0 / (GAMMA - SIGMA2)
STEP1 = (SIGMA1 / UPPER_HALF, None)
STEP2 = (2.0 * SIGMA2 / UPPER_HALF, SIGMA1 * SIGMA2)
STEP3 = (2.0 * SIGMA3 / UPPER_HALF, SIGMA2 * SIGMA3)

W = 6
F32 = jnp.float32
BF16 = jnp.bfloat16
SLOTS = ((0, 0), (0, 1), (3, 0), (3, 1), (-3, 0), (-3, 1))


END_SLOTS = ((0, None), (3, 0), (3, 1), (1, 0), (1, 1), (4, None), (-2, 0), (-2, 1))


def circulant(n):
    dense = np.zeros((n, n), np.float64)
    for k in range(1, W + 1):
        for i in range(n):
            dense[i, (i + k) % n] += COEFS[k] / COEFS[1]
            dense[i, (i - k) % n] += COEFS[k] / COEFS[1]
    high = dense.astype(ml_dtypes.bfloat16)
    low = (dense - high.astype(np.float64)).astype(ml_dtypes.bfloat16)
    return np.block([[high, low], [high, low]])


def in_planes(planes, left, right, out):
    n = left.shape[0] // 2
    for i in range(0, len(planes), 2):
        pair = [planes[i][...], planes[i + 1][...]]
        high = [f.astype(BF16) for f in pair]
        low = [(f - h.astype(F32)).astype(BF16) for f, h in zip(pair, high)]
        tall = jnp.concatenate([jnp.concatenate(high, 1), jnp.concatenate(low, 1)], 0)
        wide = jnp.concatenate([jnp.concatenate(high, 0), jnp.concatenate(low, 0)], 1)
        along_y = jnp.dot(left[...], tall, preferred_element_type=F32)
        along_z = jnp.dot(wide, right[...], preferred_element_type=F32)
        along_y = along_y[:n] + along_y[n:]
        along_z = along_z[:, :n] + along_z[:, n:]
        out[i] = KIN[1] * (along_y[:, :n] + along_z[:n])
        out[i + 1] = KIN[1] * (along_y[:, n:] + along_z[n:])


def over_tiles(n, body):
    def step(t, carry):
        body(pl.ds(pl.multiple_of(t * 8, 8), 8))
        return carry

    lax.fori_loop(0, n // 8, step, 0)


def along_x(vals, at, scale, total):
    for k in range(1, W + 1):
        below, above = vals.get(at - k), vals.get(at + k)
        if below is None and above is None:
            continue
        near = above if below is None else (below if above is None else below + above)
        total = total + (scale * KIN[k]) * near
    return total


def place(ref, i, steps, dh, way, out, first, planes):
    me = lax.axis_index("band")
    zz = lax.rem(me // 4 + way * steps + 8, 8)
    rows = pl.ds(pl.multiple_of(zz * 16 + (((me // 2) + dh) % 2) * 8, 8), 8)
    for p in range(planes):
        out[first + p, rows, :] = ref[i, p]


def kernel_place(mine, got, others, vown):
    way = 1 - 2 * (lax.axis_index("band") % 2)
    for ref, shift, turn in ((mine, 0, 1), (got, 1, 1), (others, -1, -1)):
        for i, (dz, dh) in enumerate(SLOTS):
            if shift + turn * dz != -4:
                place(ref, i, shift + turn * dz, dh, way, vown, 0, 16)


def kernel_own(x, left, right, w1, flat):
    in_planes([x.at[p] for p in range(16)], left, right, flat)

    def body(rows):
        vals = {p: x[p, rows, :] for p in range(16)}
        for p in range(16):
            total = flat[p, rows, :] + (3.0 * KIN[0] - CENTER) * vals[p]
            w1[p, rows, :] = along_x(vals, p, 1.0, total)

    over_tiles(x.shape[1], body)


def kernel_first(x, w1, xl, xr, vown, y1, to_left, to_right):
    alpha = STEP1[0]

    def body(rows):
        vals = {p - 12: xl[p, rows, :] for p in range(6, 12)}
        vals.update({p + 16: xr[p, rows, :] for p in range(6)})
        for p in range(16):
            total = w1[p, rows, :] + vown[p, rows, :] * x[p, rows, :]
            value = alpha * along_x(vals, p, 1.0, total)
            y1[p, rows, :] = value
            if 6 <= p < 12:
                to_left[p - 6, rows, :] = value
            if 4 <= p < 10:
                to_right[p - 4, rows, :] = value

    over_tiles(x.shape[1], body)


def kernel_before(x, xl, xr, y1, left, right, vown, side, y2, flat):
    n = x.shape[1]
    in_planes([xl.at[p + 6] for p in range(6)] + [xr.at[p] for p in range(6)], left, right, flat)

    def first_sides(rows):
        for s, start in enumerate((-6, 16)):
            vals = {
                p: xl[p + 12, rows, :] if p < 0 else (x[p, rows, :] if p < 16 else xr[p - 16, rows, :])
                for p in range(start - 6, start + 12)
            }
            for j in range(6):
                total = flat[6 * s + j, rows, :] + (3.0 * KIN[0] - CENTER) * vals[start + j]
                side[6 * s + j, rows, :] = along_x(vals, start + j, 1.0, total)

    over_tiles(n, first_sides)
    alpha, beta = STEP2
    in_planes([y1.at[p] for p in range(16)], left, right, flat)

    def second(rows):
        vals = {p: y1[p, rows, :] for p in range(16)}
        for p in range(16):
            total = flat[p, rows, :] + (vown[p, rows, :] + (3.0 * KIN[0] - CENTER)) * vals[p]
            y2[p, rows, :] = alpha * along_x(vals, p, 1.0, total) - beta * x[p, rows, :]

    over_tiles(n, second)


def kernel_middle(
    xl, xr, y1, left, right, vown, ends_l, ends_r, twin_l, twin_r, side, y2own, y2l, y2r, y3, y1s, y2, vs, flat
):
    n = y1.shape[1]
    core = lax.axis_index("band") % 2
    for refs, c in (((ends_l, ends_r), core), ((twin_l, twin_r), 1 - core)):
        for side_at, ref in enumerate(refs):
            for i, (steps, dh) in enumerate(END_SLOTS):
                place(ref, i, steps, c if dh is None else dh, 1 - 2 * c, vs, 6 * side_at, 6)

    def first(rows):
        for j in range(12):
            old = xl[6 + j, rows, :] if j < 6 else xr[j - 6, rows, :]
            y1s[j, rows, :] = STEP1[0] * (side[j, rows, :] + vs[j, rows, :] * old)

    over_tiles(n, first)
    alpha, beta = STEP2

    def second(rows):
        vals = {j - 6: y1s[j, rows, :] for j in range(6)}
        vals.update({j + 16: y1s[6 + j, rows, :] for j in range(6)})
        for p in range(16):
            y2[p, rows, :] = along_x(vals, p, alpha, y2own[p, rows, :])

    over_tiles(n, second)
    in_planes([y1s.at[p] for p in range(12)], left, right, flat)

    def second_sides(rows):
        for s, (start, low, top, dest, older) in enumerate(((-6, -6, 6, y2l, xl), (16, 10, 22, y2r, xr))):
            vals = {
                p: y1s[p + 6, rows, :] if p < 0 else (y1[p, rows, :] if p < 16 else y1s[p - 10, rows, :])
                for p in range(low, top)
            }
            for j in range(6):
                mid = vals[start + j]
                total = flat[6 * s + j, rows, :] + (vs[6 * s + j, rows, :] + (3.0 * KIN[0] - CENTER)) * mid
                old = older[j + 6 - 6 * s, rows, :]
                dest[j, rows, :] = alpha * along_x(vals, start + j, 1.0, total) - beta * old

    over_tiles(n, second_sides)
    alpha3, beta3 = STEP3
    in_planes([y2.at[p] for p in range(16)], left, right, flat)

    def third(rows):
        vals = {p: y2[p, rows, :] for p in range(16)}
        for p in range(16):
            total = flat[p, rows, :] + (vown[p, rows, :] + (3.0 * KIN[0] - CENTER)) * vals[p]
            y3[p, rows, :] = alpha3 * along_x(vals, p, 1.0, total) - beta3 * y1[p, rows, :]

    over_tiles(n, third)


def kernel_last(far_l, far_r, y2l, y2r, y3, out):
    def body(rows):
        far = {p - 12: far_l[p, rows, :] for p in range(6)}
        far.update({p + 22: far_r[p, rows, :] for p in range(6)})
        near = {}
        for j in range(6):
            near[j - 6] = along_x(far, j - 6, STEP2[0], y2l[j, rows, :])
            near[j + 16] = along_x(far, j + 16, STEP2[0], y2r[j, rows, :])
        for p in range(16):
            out[p, rows, :] = along_x(near, p, STEP3[0], y3[p, rows, :])

    over_tiles(out.shape[1], body)


def call(body, outs, scratch, args, flops):
    whole = pl.BlockSpec(memory_space=pltpu.VMEM)
    total = sum(a.size * a.dtype.itemsize for a in args) + sum(4 * int(np.prod(o)) for o in outs)
    return pl.pallas_call(
        body,
        out_shape=tuple(jax.ShapeDtypeStruct(o, F32) for o in outs),
        in_specs=[whole] * len(args),
        out_specs=tuple(whole for _ in outs),
        scratch_shapes=[pltpu.VMEM(s, F32) for s in scratch],
        compiler_params=pltpu.CompilerParams(vmem_limit_bytes=40 * 1024 * 1024),
        cost_estimate=pl.CostEstimate(flops=flops, bytes_accessed=total if flops else 0, transcendentals=0),
    )(*args)


def shards(orbital, potential):
    x = orbital[0]
    nx, ny, nz = x.shape
    bands, slabs = lax.axis_size("band"), lax.axis_size("slab")
    up = [(i, (i + 1) % slabs) for i in range(slabs)]
    down = [(b, a) for a, b in up]

    def of_band(value, source):
        return lax.ppermute(value, "band", [(source(i // 4, i // 2 % 2, i % 2), i) for i in range(bands)])

    def at(z, h, c):
        return z % (bands // 4) * 4 + h * 2 + c

    def flip(value):
        return of_band(value, lambda z, h, c: at(z, h, 1 - c))

    plane = (ny, nz)
    six, own, three = (6, *plane), (16, *plane), (3, *plane)
    cells = nx * ny * nz
    mat = circulant(ny)
    right = jnp.asarray(mat)
    left = jnp.asarray(np.ascontiguousarray(mat.T))
    core0 = lax.axis_index("band") % 2 == 0

    def in_order(mine, other, axis):
        return jnp.where(core0, jnp.concatenate([mine, other], axis), jnp.concatenate([other, mine], axis))

    block = in_order(potential, flip(potential), 1)
    last, first, held, block = lax.optimization_barrier((x[nx - 12 :], x[:12], x, block))
    part = of_band(jnp.where(core0, block[:8], block[8:]), lambda z, h, c: at(z, 1 - h, c))
    across = of_band(block, lambda z, h, c: at(z + 3 - 6 * c, 1 - h, c))
    along = of_band(block, lambda z, h, c: at(z + 3 - 6 * c, h, c))
    xl = lax.ppermute(last, "slab", up)
    xr = lax.ppermute(first, "slab", down)
    pieces = jnp.concatenate([along, across, part], 0)
    (w1,) = call(kernel_own, [own], [own], [held, left, right], 20000 * cells)
    pieces, w1 = lax.optimization_barrier((pieces, w1))
    twins = jnp.concatenate([flip(pieces[:16]), flip(pieces[16:])], 0)
    mine = jnp.stack(
        [block, in_order(part, twins[32:], 0), along, across, twins[:16], twins[16:32]], 0
    )
    gots = [of_band(mine[i : i + 2], lambda z, h, c: at(z + 1 - 2 * c, h, c)) for i in range(0, 6, 2)]
    got = jnp.concatenate(gots, 0)
    others = jnp.concatenate([flip(g) for g in gots], 0)
    xl, xr, others = lax.optimization_barrier((xl, xr, others))
    (vown,) = call(kernel_place, [own], [], [mine, got, others], 0)
    ends = jnp.stack(
        [
            jnp.where(core0, mine[0], mine[1]),
            mine[2],
            mine[3],
            got[0],
            got[1],
            jnp.where(core0, got[2], got[3]),
            got[4],
            got[5],
        ],
        0,
    )
    ends_l, ends_r = lax.ppermute(ends[:, nx - W :], "slab", up), lax.ppermute(ends[:, :W], "slab", down)

    y1, to_left, to_right = call(kernel_first, [own, six, six], [], [x, w1, xl, xr, vown], 0)
    far_r = lax.ppermute(to_left, "slab", down)
    far_l = lax.ppermute(to_right, "slab", up)
    twelve = (12, *plane)
    side, y2own = call(
        kernel_before, [twelve, own], [own], [x, xl, xr, y1, left, right, vown], 0
    )
    y2l, y2r, y3 = call(
        kernel_middle,
        [six, six, own],
        [twelve, own, twelve, own],
        [xl, xr, y1, left, right, vown, ends_l, ends_r, flip(ends_l), flip(ends_r), side, y2own],
        0,
    )
    (out,) = call(kernel_last, [own], [], [far_l, far_r, y2l, y2r, y3], 10 * cells)
    return out[None]


def solution(mesh):
    placed = (P("band", "slab", None, None), P("slab", "band", None))
    return jax.shard_map(
        shards, mesh=mesh, in_specs=placed, out_specs=P("band", "slab", None, None), check_vma=False
    )
```

```python
import jax
import jax.numpy as jnp
import ml_dtypes
import numpy as np
from jax import lax
from jax.experimental import pallas as pl
from jax.experimental.pallas import tpu as pltpu
from jax.sharding import PartitionSpec as P

DEGREE = 3
COEFS = (
    -5369.0 / 1800.0,
    12.0 / 7.0,
    -15.0 / 56.0,
    10.0 / 189.0,
    -1.0 / 112.0,
    2.0 / 1925.0,
    -1.0 / 16632.0,
)
INVERSE_SQ = 1.0 / 0.64
UPPER_HALF = 10.0
CENTER = 10.0
FLOOR = -5.0

KIN = tuple(-0.5 * INVERSE_SQ * c for c in COEFS)
SIGMA1 = UPPER_HALF / (FLOOR - CENTER)
GAMMA = 2.0 / SIGMA1
SIGMA2 = 1.0 / (GAMMA - SIGMA1)
SIGMA3 = 1.0 / (GAMMA - SIGMA2)
STEP1 = (SIGMA1 / UPPER_HALF, None)
STEP2 = (2.0 * SIGMA2 / UPPER_HALF, SIGMA1 * SIGMA2)
STEP3 = (2.0 * SIGMA3 / UPPER_HALF, SIGMA2 * SIGMA3)

W = 6
F32 = jnp.float32
BF16 = jnp.bfloat16
SLOTS = ((0, 0), (0, 1), (3, 0), (3, 1), (-3, 0), (-3, 1))


END_SLOTS = ((0, None), (3, 0), (3, 1), (1, 0), (1, 1), (4, None), (-2, 0), (-2, 1))


def circulant(n):
    dense = np.zeros((n, n), np.float64)
    for k in range(1, W + 1):
        for i in range(n):
            dense[i, (i + k) % n] += COEFS[k] / COEFS[1]
            dense[i, (i - k) % n] += COEFS[k] / COEFS[1]
    high = dense.astype(ml_dtypes.bfloat16)
    low = (dense - high.astype(np.float64)).astype(ml_dtypes.bfloat16)
    return np.block([[high, low], [high, low]])


def in_planes(planes, left, right, out):
    n = left.shape[0] // 2
    for i in range(0, len(planes), 2):
        pair = [planes[i][...], planes[i + 1][...]]
        high = [f.astype(BF16) for f in pair]
        low = [(f - h.astype(F32)).astype(BF16) for f, h in zip(pair, high)]
        tall = jnp.concatenate([jnp.concatenate(high, 1), jnp.concatenate(low, 1)], 0)
        wide = jnp.concatenate([jnp.concatenate(high, 0), jnp.concatenate(low, 0)], 1)
        along_y = jnp.dot(left[...], tall, preferred_element_type=F32)
        along_z = jnp.dot(wide, right[...], preferred_element_type=F32)
        along_y = along_y[:n] + along_y[n:]
        along_z = along_z[:, :n] + along_z[:, n:]
        out[i] = KIN[1] * (along_y[:, :n] + along_z[:n])
        out[i + 1] = KIN[1] * (along_y[:, n:] + along_z[n:])


def over_tiles(n, body):
    def step(t, carry):
        body(pl.ds(pl.multiple_of(t * 8, 8), 8))
        return carry

    lax.fori_loop(0, n // 8, step, 0)


def along_x(vals, at, scale, total):
    for k in range(1, W + 1):
        below, above = vals.get(at - k), vals.get(at + k)
        if below is None and above is None:
            continue
        near = above if below is None else (below if above is None else below + above)
        total = total + (scale * KIN[k]) * near
    return total


def place(ref, i, steps, dh, way, out, first, planes):
    me = lax.axis_index("band")
    zz = lax.rem(me // 4 + way * steps + 8, 8)
    rows = pl.ds(pl.multiple_of(zz * 16 + (((me // 2) + dh) % 2) * 8, 8), 8)
    for p in range(planes):
        out[first + p, rows, :] = ref[i, p]


def kernel_place(mine, got, others, vown):
    way = 1 - 2 * (lax.axis_index("band") % 2)
    for ref, shift, turn in ((mine, 0, 1), (got, 1, 1), (others, -1, -1)):
        for i, (dz, dh) in enumerate(SLOTS):
            if shift + turn * dz != -4:
                place(ref, i, shift + turn * dz, dh, way, vown, 0, 16)


def kernel_own(x, left, right, w1, flat):
    in_planes([x.at[p] for p in range(16)], left, right, flat)

    def body(rows):
        vals = {p: x[p, rows, :] for p in range(16)}
        for p in range(16):
            total = flat[p, rows, :] + (3.0 * KIN[0] - CENTER) * vals[p]
            w1[p, rows, :] = along_x(vals, p, 1.0, total)

    over_tiles(x.shape[1], body)


def kernel_first(x, w1, xl, xr, vown, y1, to_left, to_right):
    alpha = STEP1[0]

    def body(rows):
        vals = {p - 12: xl[p, rows, :] for p in range(6, 12)}
        vals.update({p + 16: xr[p, rows, :] for p in range(6)})
        for p in range(16):
            total = w1[p, rows, :] + vown[p, rows, :] * x[p, rows, :]
            value = alpha * along_x(vals, p, 1.0, total)
            y1[p, rows, :] = value
            if 6 <= p < 12:
                to_left[p - 6, rows, :] = value
            if 4 <= p < 10:
                to_right[p - 4, rows, :] = value

    over_tiles(x.shape[1], body)


def kernel_before(x, xl, xr, y1, left, right, vown, side, y2, flat):
    n = x.shape[1]
    in_planes([xl.at[p + 6] for p in range(6)] + [xr.at[p] for p in range(6)], left, right, flat)

    def first_sides(rows):
        for s, start in enumerate((-6, 16)):
            vals = {
                p: xl[p + 12, rows, :] if p < 0 else (x[p, rows, :] if p < 16 else xr[p - 16, rows, :])
                for p in range(start - 6, start + 12)
            }
            for j in range(6):
                total = flat[6 * s + j, rows, :] + (3.0 * KIN[0] - CENTER) * vals[start + j]
                side[6 * s + j, rows, :] = along_x(vals, start + j, 1.0, total)

    over_tiles(n, first_sides)
    alpha, beta = STEP2
    in_planes([y1.at[p] for p in range(16)], left, right, flat)

    def second(rows):
        vals = {p: y1[p, rows, :] for p in range(16)}
        for p in range(16):
            total = flat[p, rows, :] + (vown[p, rows, :] + (3.0 * KIN[0] - CENTER)) * vals[p]
            y2[p, rows, :] = alpha * along_x(vals, p, 1.0, total) - beta * x[p, rows, :]

    over_tiles(n, second)


def kernel_middle(
    xl, xr, y1, left, right, vown, ends_l, ends_r, twin_l, twin_r, side, y2own, y2l, y2r, y3, y1s, y2, vs, flat
):
    n = y1.shape[1]
    core = lax.axis_index("band") % 2
    for refs, c in (((ends_l, ends_r), core), ((twin_l, twin_r), 1 - core)):
        for side_at, ref in enumerate(refs):
            for i, (steps, dh) in enumerate(END_SLOTS):
                place(ref, i, steps, c if dh is None else dh, 1 - 2 * c, vs, 6 * side_at, 6)

    def first(rows):
        for j in range(12):
            old = xl[6 + j, rows, :] if j < 6 else xr[j - 6, rows, :]
            y1s[j, rows, :] = STEP1[0] * (side[j, rows, :] + vs[j, rows, :] * old)

    over_tiles(n, first)
    alpha, beta = STEP2

    def second(rows):
        vals = {j - 6: y1s[j, rows, :] for j in range(6)}
        vals.update({j + 16: y1s[6 + j, rows, :] for j in range(6)})
        for p in range(16):
            y2[p, rows, :] = along_x(vals, p, alpha, y2own[p, rows, :])

    over_tiles(n, second)
    in_planes([y1s.at[p] for p in range(12)], left, right, flat)

    def second_sides(rows):
        for s, (start, low, top, dest, older) in enumerate(((-6, -6, 6, y2l, xl), (16, 10, 22, y2r, xr))):
            vals = {
                p: y1s[p + 6, rows, :] if p < 0 else (y1[p, rows, :] if p < 16 else y1s[p - 10, rows, :])
                for p in range(low, top)
            }
            for j in range(6):
                mid = vals[start + j]
                total = flat[6 * s + j, rows, :] + (vs[6 * s + j, rows, :] + (3.0 * KIN[0] - CENTER)) * mid
                old = older[j + 6 - 6 * s, rows, :]
                dest[j, rows, :] = alpha * along_x(vals, start + j, 1.0, total) - beta * old

    over_tiles(n, second_sides)
    alpha3, beta3 = STEP3
    in_planes([y2.at[p] for p in range(16)], left, right, flat)

    def third(rows):
        vals = {p: y2[p, rows, :] for p in range(16)}
        for p in range(16):
            total = flat[p, rows, :] + (vown[p, rows, :] + (3.0 * KIN[0] - CENTER)) * vals[p]
            y3[p, rows, :] = alpha3 * along_x(vals, p, 1.0, total) - beta3 * y1[p, rows, :]

    over_tiles(n, third)


def kernel_last(far_l, far_r, y2l, y2r, y3, out, done, sems):
    def leave(source, start, stop, at):
        copy = pltpu.make_async_copy(source.at[start:stop], out.at[start:stop], sems.at[at])
        copy.start()
        return copy

    def side(far_ref, far_start, y2_ref, y2_start, first, last):
        def body(rows):
            far = {far_start + j: far_ref[j, rows, :] for j in range(W)}
            near = {y2_start + j: along_x(far, y2_start + j, STEP2[0], y2_ref[j, rows, :]) for j in range(W)}
            for p in range(first, last):
                done[p, rows, :] = along_x(near, p, STEP3[0], y3[p, rows, :])

        over_tiles(done.shape[1], body)

    copies = [leave(y3, W, 16 - W, 0)]
    side(far_l, -12, y2l, -6, 0, W)
    copies.append(leave(done, 0, W, 1))
    side(far_r, 22, y2r, 16, 16 - W, 16)
    copies.append(leave(done, 16 - W, 16, 2))
    for copy in copies:
        copy.wait()


def call(body, outs, scratch, args, flops):
    whole = pl.BlockSpec(memory_space=pltpu.VMEM)
    total = sum(a.size * a.dtype.itemsize for a in args) + sum(4 * int(np.prod(o)) for o in outs)
    return pl.pallas_call(
        body,
        out_shape=tuple(jax.ShapeDtypeStruct(o, F32) for o in outs),
        in_specs=[whole] * len(args),
        out_specs=tuple(whole for _ in outs),
        scratch_shapes=[pltpu.VMEM(s, F32) for s in scratch],
        compiler_params=pltpu.CompilerParams(vmem_limit_bytes=40 * 1024 * 1024),
        cost_estimate=pl.CostEstimate(flops=flops, bytes_accessed=total if flops else 0, transcendentals=0),
    )(*args)


def shards(orbital, potential):
    x = orbital[0]
    nx, ny, nz = x.shape
    bands, slabs = lax.axis_size("band"), lax.axis_size("slab")
    up = [(i, (i + 1) % slabs) for i in range(slabs)]
    down = [(b, a) for a, b in up]

    def of_band(value, source):
        return lax.ppermute(value, "band", [(source(i // 4, i // 2 % 2, i % 2), i) for i in range(bands)])

    def at(z, h, c):
        return z % (bands // 4) * 4 + h * 2 + c

    def flip(value):
        return of_band(value, lambda z, h, c: at(z, h, 1 - c))

    plane = (ny, nz)
    six, own, three = (6, *plane), (16, *plane), (3, *plane)
    cells = nx * ny * nz
    mat = circulant(ny)
    right = jnp.asarray(mat)
    left = jnp.asarray(np.ascontiguousarray(mat.T))
    core0 = lax.axis_index("band") % 2 == 0

    def in_order(mine, other, axis):
        return jnp.where(core0, jnp.concatenate([mine, other], axis), jnp.concatenate([other, mine], axis))

    block = in_order(potential, flip(potential), 1)
    last, first, held, block = lax.optimization_barrier((x[nx - 12 :], x[:12], x, block))
    part = of_band(jnp.where(core0, block[:8], block[8:]), lambda z, h, c: at(z, 1 - h, c))
    across = of_band(block, lambda z, h, c: at(z + 3 - 6 * c, 1 - h, c))
    along = of_band(block, lambda z, h, c: at(z + 3 - 6 * c, h, c))
    xl = lax.ppermute(last, "slab", up)
    xr = lax.ppermute(first, "slab", down)
    pieces = jnp.concatenate([along, across, part], 0)
    (w1,) = call(kernel_own, [own], [own], [held, left, right], 20000 * cells)
    pieces, w1 = lax.optimization_barrier((pieces, w1))
    twins = jnp.concatenate([flip(pieces[:16]), flip(pieces[16:])], 0)
    mine = jnp.stack(
        [block, in_order(part, twins[32:], 0), along, across, twins[:16], twins[16:32]], 0
    )
    gots = [of_band(mine[i : i + 2], lambda z, h, c: at(z + 1 - 2 * c, h, c)) for i in range(0, 6, 2)]
    got = jnp.concatenate(gots, 0)
    others = jnp.concatenate([flip(g) for g in gots], 0)
    xl, xr, others = lax.optimization_barrier((xl, xr, others))
    (vown,) = call(kernel_place, [own], [], [mine, got, others], 0)
    ends = jnp.stack(
        [
            jnp.where(core0, mine[0], mine[1]),
            mine[2],
            mine[3],
            got[0],
            got[1],
            jnp.where(core0, got[2], got[3]),
            got[4],
            got[5],
        ],
        0,
    )
    ends_l, ends_r = lax.ppermute(ends[:, nx - W :], "slab", up), lax.ppermute(ends[:, :W], "slab", down)

    y1, to_left, to_right = call(kernel_first, [own, six, six], [], [x, w1, xl, xr, vown], 0)
    far_r = lax.ppermute(to_left, "slab", down)
    far_l = lax.ppermute(to_right, "slab", up)
    twelve = (12, *plane)
    side, y2own = call(
        kernel_before, [twelve, own], [own], [x, xl, xr, y1, left, right, vown], 0
    )
    y2l, y2r, y3 = call(
        kernel_middle,
        [six, six, own],
        [twelve, own, twelve, own],
        [xl, xr, y1, left, right, vown, ends_l, ends_r, flip(ends_l), flip(ends_r), side, y2own],
        0,
    )
    out = pl.pallas_call(
        kernel_last,
        out_shape=jax.ShapeDtypeStruct(own, F32),
        in_specs=[pl.BlockSpec(memory_space=pltpu.VMEM)] * 5,
        out_specs=pl.BlockSpec(memory_space=pl.ANY),
        scratch_shapes=[pltpu.VMEM(own, F32), pltpu.SemaphoreType.DMA((3,))],
        compiler_params=pltpu.CompilerParams(vmem_limit_bytes=40 * 1024 * 1024),
        cost_estimate=pl.CostEstimate(flops=10 * cells, bytes_accessed=8 * cells, transcendentals=0),
    )(far_l, far_r, y2l, y2r, y3)
    return out[None]


def solution(mesh):
    placed = (P("band", "slab", None, None), P("slab", "band", None))
    return jax.shard_map(
        shards, mesh=mesh, in_specs=placed, out_specs=P("band", "slab", None, None), check_vma=False
    )
```

```python
import jax
import jax.numpy as jnp
import ml_dtypes
import numpy as np
from jax import lax
from jax.experimental import pallas as pl
from jax.experimental.pallas import tpu as pltpu
from jax.sharding import PartitionSpec as P

DEGREE = 3
COEFS = (
    -5369.0 / 1800.0,
    12.0 / 7.0,
    -15.0 / 56.0,
    10.0 / 189.0,
    -1.0 / 112.0,
    2.0 / 1925.0,
    -1.0 / 16632.0,
)
INVERSE_SQ = 1.0 / 0.64
UPPER_HALF = 10.0
CENTER = 10.0
FLOOR = -5.0

KIN = tuple(-0.5 * INVERSE_SQ * c for c in COEFS)
SIGMA1 = UPPER_HALF / (FLOOR - CENTER)
GAMMA = 2.0 / SIGMA1
SIGMA2 = 1.0 / (GAMMA - SIGMA1)
SIGMA3 = 1.0 / (GAMMA - SIGMA2)
STEP1 = (SIGMA1 / UPPER_HALF, None)
STEP2 = (2.0 * SIGMA2 / UPPER_HALF, SIGMA1 * SIGMA2)
STEP3 = (2.0 * SIGMA3 / UPPER_HALF, SIGMA2 * SIGMA3)

W = 6
F32 = jnp.float32
BF16 = jnp.bfloat16
SLOTS = ((0, 0), (0, 1), (3, 0), (3, 1), (-3, 0), (-3, 1))


END_SLOTS = ((0, None), (3, 0), (3, 1), (1, 0), (1, 1), (4, None), (-2, 0), (-2, 1))


def circulant(n):
    dense = np.zeros((n, n), np.float64)
    for k in range(1, W + 1):
        for i in range(n):
            dense[i, (i + k) % n] += COEFS[k] / COEFS[1]
            dense[i, (i - k) % n] += COEFS[k] / COEFS[1]
    high = dense.astype(ml_dtypes.bfloat16)
    low = (dense - high.astype(np.float64)).astype(ml_dtypes.bfloat16)
    return np.block([[high, low], [high, low]])


def in_planes(planes, left, right, out):
    n = left.shape[0] // 2
    for i in range(0, len(planes), 2):
        pair = [planes[i][...], planes[i + 1][...]]
        high = [f.astype(BF16) for f in pair]
        low = [(f - h.astype(F32)).astype(BF16) for f, h in zip(pair, high)]
        tall = jnp.concatenate([jnp.concatenate(high, 1), jnp.concatenate(low, 1)], 0)
        wide = jnp.concatenate([jnp.concatenate(high, 0), jnp.concatenate(low, 0)], 1)
        along_y = jnp.dot(left[...], tall, preferred_element_type=F32)
        along_z = jnp.dot(wide, right[...], preferred_element_type=F32)
        along_y = along_y[:n] + along_y[n:]
        along_z = along_z[:, :n] + along_z[:, n:]
        out[i] = KIN[1] * (along_y[:, :n] + along_z[:n])
        out[i + 1] = KIN[1] * (along_y[:, n:] + along_z[n:])


def over_tiles(n, body):
    def step(t, carry):
        body(pl.ds(pl.multiple_of(t * 8, 8), 8))
        return carry

    lax.fori_loop(0, n // 8, step, 0)


def along_x(vals, at, scale, total):
    for k in range(1, W + 1):
        below, above = vals.get(at - k), vals.get(at + k)
        if below is None and above is None:
            continue
        near = above if below is None else (below if above is None else below + above)
        total = total + (scale * KIN[k]) * near
    return total


def place(ref, i, steps, dh, way, out, first, planes):
    me = lax.axis_index("band")
    zz = lax.rem(me // 4 + way * steps + 8, 8)
    rows = pl.ds(pl.multiple_of(zz * 16 + (((me // 2) + dh) % 2) * 8, 8), 8)
    for p in range(planes):
        out[first + p, rows, :] = ref[i, p]


def kernel_place(mine, got, others, vown):
    core = lax.axis_index("band") % 2
    for i, (steps, dh) in enumerate(SLOTS):
        place(mine, i, steps, dh, 1 - 2 * core, vown, 0, 16)
    for ref, c in ((got, core), (others, 1 - core)):
        for i, (steps, dh) in enumerate(END_SLOTS[3:]):
            place(ref, i, steps, c if dh is None else dh, 1 - 2 * c, vown, 0, 16)


def kernel_own(x, left, right, w1, flat):
    in_planes([x.at[p] for p in range(16)], left, right, flat)

    def body(rows):
        vals = {p: x[p, rows, :] for p in range(16)}
        for p in range(16):
            total = flat[p, rows, :] + (3.0 * KIN[0] - CENTER) * vals[p]
            w1[p, rows, :] = along_x(vals, p, 1.0, total)

    over_tiles(x.shape[1], body)


def kernel_first(x, w1, xl, xr, vown, y1, to_left, to_right):
    alpha = STEP1[0]

    def body(rows):
        vals = {p - 12: xl[p, rows, :] for p in range(6, 12)}
        vals.update({p + 16: xr[p, rows, :] for p in range(6)})
        for p in range(16):
            total = w1[p, rows, :] + vown[p, rows, :] * x[p, rows, :]
            value = alpha * along_x(vals, p, 1.0, total)
            y1[p, rows, :] = value
            if 6 <= p < 12:
                to_left[p - 6, rows, :] = value
            if 4 <= p < 10:
                to_right[p - 4, rows, :] = value

    over_tiles(x.shape[1], body)


def kernel_before(x, xl, xr, y1, left, right, vown, side, y2, flat):
    n = x.shape[1]
    in_planes([xl.at[p + 6] for p in range(6)] + [xr.at[p] for p in range(6)], left, right, flat)

    def first_sides(rows):
        for s, start in enumerate((-6, 16)):
            vals = {
                p: xl[p + 12, rows, :] if p < 0 else (x[p, rows, :] if p < 16 else xr[p - 16, rows, :])
                for p in range(start - 6, start + 12)
            }
            for j in range(6):
                total = flat[6 * s + j, rows, :] + (3.0 * KIN[0] - CENTER) * vals[start + j]
                side[6 * s + j, rows, :] = along_x(vals, start + j, 1.0, total)

    over_tiles(n, first_sides)
    alpha, beta = STEP2
    in_planes([y1.at[p] for p in range(16)], left, right, flat)

    def second(rows):
        vals = {p: y1[p, rows, :] for p in range(16)}
        for p in range(16):
            total = flat[p, rows, :] + (vown[p, rows, :] + (3.0 * KIN[0] - CENTER)) * vals[p]
            y2[p, rows, :] = alpha * along_x(vals, p, 1.0, total) - beta * x[p, rows, :]

    over_tiles(n, second)


def kernel_middle(
    xl, xr, y1, left, right, vown, ends_l, ends_r, twin_l, twin_r, side, y2own, y2l, y2r, y3, y1s, y2, vs, flat
):
    n = y1.shape[1]
    core = lax.axis_index("band") % 2
    for refs, c in (((ends_l, ends_r), core), ((twin_l, twin_r), 1 - core)):
        for side_at, ref in enumerate(refs):
            for i, (steps, dh) in enumerate(END_SLOTS):
                place(ref, i, steps, c if dh is None else dh, 1 - 2 * c, vs, 6 * side_at, 6)

    def first(rows):
        for j in range(12):
            old = xl[6 + j, rows, :] if j < 6 else xr[j - 6, rows, :]
            y1s[j, rows, :] = STEP1[0] * (side[j, rows, :] + vs[j, rows, :] * old)

    over_tiles(n, first)
    alpha, beta = STEP2

    def second(rows):
        vals = {j - 6: y1s[j, rows, :] for j in range(6)}
        vals.update({j + 16: y1s[6 + j, rows, :] for j in range(6)})
        for p in range(16):
            y2[p, rows, :] = along_x(vals, p, alpha, y2own[p, rows, :])

    over_tiles(n, second)
    in_planes([y1s.at[p] for p in range(12)], left, right, flat)

    def second_sides(rows):
        for s, (start, low, top, dest, older) in enumerate(((-6, -6, 6, y2l, xl), (16, 10, 22, y2r, xr))):
            vals = {
                p: y1s[p + 6, rows, :] if p < 0 else (y1[p, rows, :] if p < 16 else y1s[p - 10, rows, :])
                for p in range(low, top)
            }
            for j in range(6):
                mid = vals[start + j]
                total = flat[6 * s + j, rows, :] + (vs[6 * s + j, rows, :] + (3.0 * KIN[0] - CENTER)) * mid
                old = older[j + 6 - 6 * s, rows, :]
                dest[j, rows, :] = alpha * along_x(vals, start + j, 1.0, total) - beta * old

    over_tiles(n, second_sides)
    alpha3, beta3 = STEP3
    in_planes([y2.at[p] for p in range(16)], left, right, flat)

    def third(rows):
        vals = {p: y2[p, rows, :] for p in range(16)}
        for p in range(16):
            total = flat[p, rows, :] + (vown[p, rows, :] + (3.0 * KIN[0] - CENTER)) * vals[p]
            y3[p, rows, :] = alpha3 * along_x(vals, p, 1.0, total) - beta3 * y1[p, rows, :]

    over_tiles(n, third)


def kernel_last(far_l, far_r, y2l, y2r, y3, out, done, sems):
    def leave(source, start, stop, at):
        copy = pltpu.make_async_copy(source.at[start:stop], out.at[start:stop], sems.at[at])
        copy.start()
        return copy

    def side(far_ref, far_start, y2_ref, y2_start, first, last):
        def body(rows):
            far = {far_start + j: far_ref[j, rows, :] for j in range(W)}
            near = {y2_start + j: along_x(far, y2_start + j, STEP2[0], y2_ref[j, rows, :]) for j in range(W)}
            for p in range(first, last):
                done[p, rows, :] = along_x(near, p, STEP3[0], y3[p, rows, :])

        over_tiles(done.shape[1], body)

    copies = [leave(y3, W, 16 - W, 0)]
    side(far_l, -12, y2l, -6, 0, W)
    copies.append(leave(done, 0, W, 1))
    side(far_r, 22, y2r, 16, 16 - W, 16)
    copies.append(leave(done, 16 - W, 16, 2))
    for copy in copies:
        copy.wait()


def call(body, outs, scratch, args, flops):
    whole = pl.BlockSpec(memory_space=pltpu.VMEM)
    total = sum(a.size * a.dtype.itemsize for a in args) + sum(4 * int(np.prod(o)) for o in outs)
    return pl.pallas_call(
        body,
        out_shape=tuple(jax.ShapeDtypeStruct(o, F32) for o in outs),
        in_specs=[whole] * len(args),
        out_specs=tuple(whole for _ in outs),
        scratch_shapes=[pltpu.VMEM(s, F32) for s in scratch],
        compiler_params=pltpu.CompilerParams(vmem_limit_bytes=40 * 1024 * 1024),
        cost_estimate=pl.CostEstimate(flops=flops, bytes_accessed=total if flops else 0, transcendentals=0),
    )(*args)


def shards(orbital, potential):
    x = orbital[0]
    nx, ny, nz = x.shape
    bands, slabs = lax.axis_size("band"), lax.axis_size("slab")
    up = [(i, (i + 1) % slabs) for i in range(slabs)]
    down = [(b, a) for a, b in up]

    def of_band(value, source):
        return lax.ppermute(value, "band", [(source(i // 4, i // 2 % 2, i % 2), i) for i in range(bands)])

    def at(z, h, c):
        return z % (bands // 4) * 4 + h * 2 + c

    def flip(value):
        return of_band(value, lambda z, h, c: at(z, h, 1 - c))

    plane = (ny, nz)
    six, own, three = (6, *plane), (16, *plane), (3, *plane)
    cells = nx * ny * nz
    mat = circulant(ny)
    right = jnp.asarray(mat)
    left = jnp.asarray(np.ascontiguousarray(mat.T))
    core0 = lax.axis_index("band") % 2 == 0

    def in_order(mine, other, axis):
        return jnp.where(core0, jnp.concatenate([mine, other], axis), jnp.concatenate([other, mine], axis))

    block = in_order(potential, flip(potential), 1)
    last, first, held, block = lax.optimization_barrier((x[nx - 12 :], x[:12], x, block))
    part = of_band(jnp.where(core0, block[:8], block[8:]), lambda z, h, c: at(z, 1 - h, c))
    across = of_band(block, lambda z, h, c: at(z + 3 - 6 * c, 1 - h, c))
    along = of_band(block, lambda z, h, c: at(z + 3 - 6 * c, h, c))
    xl = lax.ppermute(last, "slab", up)
    xr = lax.ppermute(first, "slab", down)
    pieces = jnp.concatenate([along, across, part], 0)
    (w1,) = call(kernel_own, [own], [own], [held, left, right], 20000 * cells)
    pieces, w1 = lax.optimization_barrier((pieces, w1))
    twins = jnp.concatenate([flip(pieces[:16]), flip(pieces[16:])], 0)
    mine = jnp.stack(
        [block, in_order(part, twins[32:], 0), along, across, twins[:16], twins[16:32]], 0
    )
    half = jnp.where(core0, mine[2:3], mine[3:4])
    gots = [of_band(part, lambda z, h, c: at(z + 1 - 2 * c, h, c)) for part in (mine[:2], jnp.concatenate([half, mine[4:]], 0))]
    got = jnp.concatenate(gots, 0)
    others = jnp.concatenate([flip(g) for g in gots], 0)
    xl, xr, others = lax.optimization_barrier((xl, xr, others))
    (vown,) = call(kernel_place, [own], [], [mine, got, others], 0)
    ends = jnp.stack(
        [
            jnp.where(core0, mine[0], mine[1]),
            mine[2],
            mine[3],
            got[0],
            got[1],
            got[2],
            got[3],
            got[4],
        ],
        0,
    )
    ends_l, ends_r = lax.ppermute(ends[:, nx - W :], "slab", up), lax.ppermute(ends[:, :W], "slab", down)

    y1, to_left, to_right = call(kernel_first, [own, six, six], [], [x, w1, xl, xr, vown], 0)
    far_r = lax.ppermute(to_left, "slab", down)
    far_l = lax.ppermute(to_right, "slab", up)
    twelve = (12, *plane)
    side, y2own = call(
        kernel_before, [twelve, own], [own], [x, xl, xr, y1, left, right, vown], 0
    )
    y2l, y2r, y3 = call(
        kernel_middle,
        [six, six, own],
        [twelve, own, twelve, own],
        [xl, xr, y1, left, right, vown, ends_l, ends_r, flip(ends_l), flip(ends_r), side, y2own],
        0,
    )
    out = pl.pallas_call(
        kernel_last,
        out_shape=jax.ShapeDtypeStruct(own, F32),
        in_specs=[pl.BlockSpec(memory_space=pltpu.VMEM)] * 5,
        out_specs=pl.BlockSpec(memory_space=pl.ANY),
        scratch_shapes=[pltpu.VMEM(own, F32), pltpu.SemaphoreType.DMA((3,))],
        compiler_params=pltpu.CompilerParams(vmem_limit_bytes=40 * 1024 * 1024),
        cost_estimate=pl.CostEstimate(flops=10 * cells, bytes_accessed=8 * cells, transcendentals=0),
    )(far_l, far_r, y2l, y2r, y3)
    return out[None]


def solution(mesh):
    placed = (P("band", "slab", None, None), P("slab", "band", None))
    return jax.shard_map(
        shards, mesh=mesh, in_specs=placed, out_specs=P("band", "slab", None, None), check_vma=False
    )
```

```python
import jax
import jax.numpy as jnp
import ml_dtypes
import numpy as np
from jax import lax
from jax.experimental import pallas as pl
from jax.experimental.pallas import tpu as pltpu
from jax.sharding import PartitionSpec as P

DEGREE = 3
COEFS = (
    -5369.0 / 1800.0,
    12.0 / 7.0,
    -15.0 / 56.0,
    10.0 / 189.0,
    -1.0 / 112.0,
    2.0 / 1925.0,
    -1.0 / 16632.0,
)
INVERSE_SQ = 1.0 / 0.64
UPPER_HALF = 10.0
CENTER = 10.0
FLOOR = -5.0

KIN = tuple(-0.5 * INVERSE_SQ * c for c in COEFS)
SIGMA1 = UPPER_HALF / (FLOOR - CENTER)
GAMMA = 2.0 / SIGMA1
SIGMA2 = 1.0 / (GAMMA - SIGMA1)
SIGMA3 = 1.0 / (GAMMA - SIGMA2)
STEP1 = (SIGMA1 / UPPER_HALF, None)
STEP2 = (2.0 * SIGMA2 / UPPER_HALF, SIGMA1 * SIGMA2)
STEP3 = (2.0 * SIGMA3 / UPPER_HALF, SIGMA2 * SIGMA3)

W = 6
F32 = jnp.float32
BF16 = jnp.bfloat16
SLOTS = ((0, 0), (0, 1), (3, 0), (3, 1), (-3, 0), (-3, 1))


END_SLOTS = ((0, None), (3, 0), (3, 1), (1, 0), (1, 1), (4, None), (-2, 0), (-2, 1))


def circulant(n):
    dense = np.zeros((n, n), np.float64)
    for k in range(1, W + 1):
        for i in range(n):
            dense[i, (i + k) % n] += COEFS[k] / COEFS[1]
            dense[i, (i - k) % n] += COEFS[k] / COEFS[1]
    high = dense.astype(ml_dtypes.bfloat16)
    low = (dense - high.astype(np.float64)).astype(ml_dtypes.bfloat16)
    return np.block([[high, low], [high, low]])


def in_planes(planes, left, right, out):
    n = left.shape[0] // 2
    for i in range(0, len(planes), 2):
        pair = [planes[i][...], planes[i + 1][...]]
        high = [f.astype(BF16) for f in pair]
        low = [(f - h.astype(F32)).astype(BF16) for f, h in zip(pair, high)]
        tall = jnp.concatenate([jnp.concatenate(high, 1), jnp.concatenate(low, 1)], 0)
        wide = jnp.concatenate([jnp.concatenate(high, 0), jnp.concatenate(low, 0)], 1)
        along_y = jnp.dot(left[...], tall, preferred_element_type=F32)
        along_z = jnp.dot(wide, right[...], preferred_element_type=F32)
        along_y = along_y[:n] + along_y[n:]
        along_z = along_z[:, :n] + along_z[:, n:]
        out[i] = KIN[1] * (along_y[:, :n] + along_z[:n])
        out[i + 1] = KIN[1] * (along_y[:, n:] + along_z[n:])


def over_tiles(n, body):
    def step(t, carry):
        body(pl.ds(pl.multiple_of(t * 8, 8), 8))
        return carry

    lax.fori_loop(0, n // 8, step, 0)


def along_x(vals, at, scale, total):
    for k in range(1, W + 1):
        below, above = vals.get(at - k), vals.get(at + k)
        if below is None and above is None:
            continue
        near = above if below is None else (below if above is None else below + above)
        total = total + (scale * KIN[k]) * near
    return total


def place(ref, i, steps, dh, way, out, first, planes):
    me = lax.axis_index("band")
    zz = lax.rem(me // 4 + way * steps + 8, 8)
    rows = pl.ds(pl.multiple_of(zz * 16 + (((me // 2) + dh) % 2) * 8, 8), 8)
    for p in range(planes):
        out[first + p, rows, :] = ref[i, p]


def kernel_place(mine, got, others, vown):
    core = lax.axis_index("band") % 2
    for i, (steps, dh) in enumerate(SLOTS):
        place(mine, i, steps, dh, 1 - 2 * core, vown, 0, 16)
    for ref, c in ((got, core), (others, 1 - core)):
        for i, (steps, dh) in enumerate(END_SLOTS[3:]):
            place(ref, i, steps, c if dh is None else dh, 1 - 2 * c, vown, 0, 16)


def kernel_own(x, left, right, w1, flat):
    in_planes([x.at[p] for p in range(16)], left, right, flat)

    def body(rows):
        vals = {p: x[p, rows, :] for p in range(16)}
        for p in range(16):
            total = flat[p, rows, :] + (3.0 * KIN[0] - CENTER) * vals[p]
            w1[p, rows, :] = along_x(vals, p, 1.0, total)

    over_tiles(x.shape[1], body)


def kernel_first(x, w1, xl, xr, vown, y1, to_left, to_right):
    alpha = STEP1[0]

    def body(rows):
        vals = {p - 12: xl[p, rows, :] for p in range(6, 12)}
        vals.update({p + 16: xr[p, rows, :] for p in range(6)})
        for p in range(16):
            total = w1[p, rows, :] + vown[p, rows, :] * x[p, rows, :]
            value = alpha * along_x(vals, p, 1.0, total)
            y1[p, rows, :] = value
            if 6 <= p < 12:
                to_left[p - 6, rows, :] = value
            if 4 <= p < 10:
                to_right[p - 4, rows, :] = value

    over_tiles(x.shape[1], body)


def kernel_before(x, xl, xr, y1, left, right, vown, side, y2, flat):
    n = x.shape[1]
    in_planes([xl.at[p + 6] for p in range(6)] + [xr.at[p] for p in range(6)], left, right, flat)

    def first_sides(rows):
        for s, start in enumerate((-6, 16)):
            vals = {
                p: xl[p + 12, rows, :] if p < 0 else (x[p, rows, :] if p < 16 else xr[p - 16, rows, :])
                for p in range(start - 6, start + 12)
            }
            for j in range(6):
                total = flat[6 * s + j, rows, :] + (3.0 * KIN[0] - CENTER) * vals[start + j]
                side[6 * s + j, rows, :] = along_x(vals, start + j, 1.0, total)

    over_tiles(n, first_sides)
    alpha, beta = STEP2
    in_planes([y1.at[p] for p in range(16)], left, right, flat)

    def second(rows):
        vals = {p: y1[p, rows, :] for p in range(16)}
        for p in range(16):
            total = flat[p, rows, :] + (vown[p, rows, :] + (3.0 * KIN[0] - CENTER)) * vals[p]
            y2[p, rows, :] = alpha * along_x(vals, p, 1.0, total) - beta * x[p, rows, :]

    over_tiles(n, second)


def kernel_middle(
    xl, xr, y1, left, right, vown, ends_l, ends_r, twin_l, twin_r, side, y2own, y2l, y2r, y3, y1s, y2, vs, flat
):
    n = y1.shape[1]
    core = lax.axis_index("band") % 2
    for refs, c in (((ends_l, ends_r), core), ((twin_l, twin_r), 1 - core)):
        for side_at, ref in enumerate(refs):
            for i, (steps, dh) in enumerate(END_SLOTS):
                place(ref, i, steps, c if dh is None else dh, 1 - 2 * c, vs, 6 * side_at, 6)

    def first(rows):
        for j in range(12):
            old = xl[6 + j, rows, :] if j < 6 else xr[j - 6, rows, :]
            y1s[j, rows, :] = STEP1[0] * (side[j, rows, :] + vs[j, rows, :] * old)

    over_tiles(n, first)
    alpha, beta = STEP2

    def second(rows):
        vals = {j - 6: y1s[j, rows, :] for j in range(6)}
        vals.update({j + 16: y1s[6 + j, rows, :] for j in range(6)})
        for p in range(16):
            y2[p, rows, :] = along_x(vals, p, alpha, y2own[p, rows, :])

    over_tiles(n, second)
    in_planes([y1s.at[p] for p in range(12)], left, right, flat)

    def second_sides(rows):
        for s, (start, low, top, dest, older) in enumerate(((-6, -6, 6, y2l, xl), (16, 10, 22, y2r, xr))):
            vals = {
                p: y1s[p + 6, rows, :] if p < 0 else (y1[p, rows, :] if p < 16 else y1s[p - 10, rows, :])
                for p in range(low, top)
            }
            for j in range(6):
                mid = vals[start + j]
                total = flat[6 * s + j, rows, :] + (vs[6 * s + j, rows, :] + (3.0 * KIN[0] - CENTER)) * mid
                old = older[j + 6 - 6 * s, rows, :]
                dest[j, rows, :] = alpha * along_x(vals, start + j, 1.0, total) - beta * old

    over_tiles(n, second_sides)
    alpha3, beta3 = STEP3
    in_planes([y2.at[p] for p in range(16)], left, right, flat)

    def third(rows):
        vals = {p: y2[p, rows, :] for p in range(16)}
        for p in range(16):
            total = flat[p, rows, :] + (vown[p, rows, :] + (3.0 * KIN[0] - CENTER)) * vals[p]
            y3[p, rows, :] = alpha3 * along_x(vals, p, 1.0, total) - beta3 * y1[p, rows, :]

    over_tiles(n, third)


def kernel_last(far_l, far_r, y2l, y2r, y3, out, done, sems):
    def leave(source, start, stop, at):
        copy = pltpu.make_async_copy(source.at[start:stop], out.at[start:stop], sems.at[at])
        copy.start()
        return copy

    def side(far_ref, far_start, y2_ref, y2_start, first, last):
        def body(rows):
            far = {far_start + j: far_ref[j, rows, :] for j in range(W)}
            near = {y2_start + j: along_x(far, y2_start + j, STEP2[0], y2_ref[j, rows, :]) for j in range(W)}
            for p in range(first, last):
                done[p, rows, :] = along_x(near, p, STEP3[0], y3[p, rows, :])

        over_tiles(done.shape[1], body)

    copies = [leave(y3, W, 16 - W, 0)]
    side(far_l, -12, y2l, -6, 0, W)
    copies.append(leave(done, 0, W, 1))
    side(far_r, 22, y2r, 16, 16 - W, 16)
    copies.append(leave(done, 16 - W, 16, 2))
    for copy in copies:
        copy.wait()


def call(body, outs, scratch, args, flops):
    whole = pl.BlockSpec(memory_space=pltpu.VMEM)
    total = sum(a.size * a.dtype.itemsize for a in args) + sum(4 * int(np.prod(o)) for o in outs)
    return pl.pallas_call(
        body,
        out_shape=tuple(jax.ShapeDtypeStruct(o, F32) for o in outs),
        in_specs=[whole] * len(args),
        out_specs=tuple(whole for _ in outs),
        scratch_shapes=[pltpu.VMEM(s, F32) for s in scratch],
        compiler_params=pltpu.CompilerParams(vmem_limit_bytes=40 * 1024 * 1024),
        cost_estimate=pl.CostEstimate(flops=flops, bytes_accessed=total if flops else 0, transcendentals=0),
    )(*args)


def shards(orbital, potential):
    x = orbital[0]
    nx, ny, nz = x.shape
    bands, slabs = lax.axis_size("band"), lax.axis_size("slab")
    up = [(i, (i + 1) % slabs) for i in range(slabs)]
    down = [(b, a) for a, b in up]

    def of_band(value, source):
        return lax.ppermute(value, "band", [(source(i // 4, i // 2 % 2, i % 2), i) for i in range(bands)])

    def at(z, h, c):
        return z % (bands // 4) * 4 + h * 2 + c

    def flip(value):
        return of_band(value, lambda z, h, c: at(z, h, 1 - c))

    plane = (ny, nz)
    six, own, three = (6, *plane), (16, *plane), (3, *plane)
    cells = nx * ny * nz
    mat = circulant(ny)
    right = jnp.asarray(mat)
    left = jnp.asarray(np.ascontiguousarray(mat.T))
    core0 = lax.axis_index("band") % 2 == 0

    def in_order(mine, other, axis):
        return jnp.where(core0, jnp.concatenate([mine, other], axis), jnp.concatenate([other, mine], axis))

    block = in_order(potential, flip(potential), 1)
    last, first, held, block = lax.optimization_barrier((x[nx - 12 :], x[:12], x, block))
    part = of_band(jnp.where(core0, block[:8], block[8:]), lambda z, h, c: at(z, 1 - h, c))
    across = of_band(block, lambda z, h, c: at(z + 3 - 6 * c, 1 - h, c))
    along = of_band(block, lambda z, h, c: at(z + 3 - 6 * c, h, c))
    xl = lax.ppermute(last, "slab", up)
    xr = lax.ppermute(first, "slab", down)
    pieces = jnp.concatenate([along, across, part], 0)
    (w1,) = call(kernel_own, [own], [own], [held, left, right], 20000 * cells)
    pieces, w1 = lax.optimization_barrier((pieces, w1))
    twins = jnp.concatenate([flip(pieces[:16]), flip(pieces[16:])], 0)
    mine = jnp.stack(
        [block, in_order(part, twins[32:], 0), along, across, twins[:16], twins[16:32]], 0
    )
    half = jnp.where(core0, mine[2:3], mine[3:4])
    gots = [of_band(part, lambda z, h, c: at(z + 1 - 2 * c, h, c)) for part in (mine[:2], jnp.concatenate([half, mine[4:5]], 0), mine[5:])]
    got = jnp.concatenate(gots, 0)
    others = jnp.concatenate([flip(g) for g in gots], 0)
    xl, xr, others = lax.optimization_barrier((xl, xr, others))
    (vown,) = call(kernel_place, [own], [], [mine, got, others], 0)
    ends = jnp.stack(
        [
            jnp.where(core0, mine[0], mine[1]),
            mine[2],
            mine[3],
            got[0],
            got[1],
            got[2],
            got[3],
            got[4],
        ],
        0,
    )
    ends_l, ends_r = lax.ppermute(ends[:, nx - W :], "slab", up), lax.ppermute(ends[:, :W], "slab", down)

    y1, to_left, to_right = call(kernel_first, [own, six, six], [], [x, w1, xl, xr, vown], 0)
    far_r = lax.ppermute(to_left, "slab", down)
    far_l = lax.ppermute(to_right, "slab", up)
    twelve = (12, *plane)
    side, y2own = call(
        kernel_before, [twelve, own], [own], [x, xl, xr, y1, left, right, vown], 0
    )
    y2l, y2r, y3 = call(
        kernel_middle,
        [six, six, own],
        [twelve, own, twelve, own],
        [xl, xr, y1, left, right, vown, ends_l, ends_r, flip(ends_l), flip(ends_r), side, y2own],
        0,
    )
    out = pl.pallas_call(
        kernel_last,
        out_shape=jax.ShapeDtypeStruct(own, F32),
        in_specs=[pl.BlockSpec(memory_space=pltpu.VMEM)] * 5,
        out_specs=pl.BlockSpec(memory_space=pl.ANY),
        scratch_shapes=[pltpu.VMEM(own, F32), pltpu.SemaphoreType.DMA((3,))],
        compiler_params=pltpu.CompilerParams(vmem_limit_bytes=40 * 1024 * 1024),
        cost_estimate=pl.CostEstimate(flops=10 * cells, bytes_accessed=8 * cells, transcendentals=0),
    )(far_l, far_r, y2l, y2r, y3)
    return out[None]


def solution(mesh):
    placed = (P("band", "slab", None, None), P("slab", "band", None))
    return jax.shard_map(
        shards, mesh=mesh, in_specs=placed, out_specs=P("band", "slab", None, None), check_vma=False
    )
```
